32 devices in a mesh: stn: 16 (over z, y, core), seg: 2 (over x).
Axes of the slice: x: 2, y: 2, z: 4, core: 2. Of those that a mesh axis runs over, the one named last changes fastest.
Arguments:
- spectra: bfloat16 [2, 32, 2, 4096], P('seg', 'stn'), may hold values from -60 to 60, as said below
- flags: int32 [32], P('stn'), may hold values 0 or 1
- pair_first: int32 [16, 16, 4], P('stn'), may hold values from 0 to 1
- pair_second: int32 [16, 16, 4], P('stn'), may hold values from 0 to 1
- owners: int32 [16, 16, 4, 1], P('stn'), may hold values from 0 to 15; in each aligned block of 64 rows (0 to 63, 64 to 127, ..., all dimensions but the last counted through in order) at most 8 rows name the same one
Outputs:
- stacks: float32 [16, 16, 8, 1024], P('stn', None, None, 'seg')
The draws below stay inside these ranges and needn't reach their ends.
Inputs may be any that keep to these rules, and one draw needn't show every extreme that they name: `spectra`: spectra of one station vary in scale from band to band. `owners`: at most 8 pairs of one source block name the same owner; in every draw some source block gives exactly 8 pairs to one owner.
All inputs are finite; a program needn't handle non-finite values. No bound on the sum of `flags` on one device may be relied on, other than what follows from the above.
Results may differ from the reference program's by a relative error of at most 0.018.
Values may be sent and summed in bfloat16 or wider, within the bound.
A program may use at most 128 MiB of HBM per device.

```python
import math
import jax
import jax.numpy as jnp
import numpy as np
from jax import lax

F = 4096
LAGS = 1024
BAND = 64
ST_DEV = 2
CAP = 4
CAPO = 8
BLOCKS = 16
STATIONS = 32
SEGS = 2


def draw_spectra(key, part):
    key = jax.random.fold_in(key, 11)
    noise_key, scale_key = jax.random.split(key)
    shape = (SEGS, STATIONS, 2, F // BAND, BAND)
    scale_shape = (SEGS, STATIONS, 1, F // BAND, 1)
    base = jnp.clip(jax.random.normal(noise_key, shape, jnp.float32), -6.0, 6.0)
    logs = jax.random.uniform(scale_key, scale_shape, jnp.float32, math.log(0.3), math.log(3.0))
    values = base * jnp.exp(logs)
    return values.reshape((SEGS, STATIONS, 2, F)).astype(jnp.bfloat16)


def place_ends(entries, rng, low, largest):
    spot = [jax.random.randint(jax.random.fold_in(rng, axis), (), 0, length) for axis, length in enumerate(entries.shape)]
    longest = entries.shape.index(max(entries.shape))
    neighbour = spot[:longest] + [(spot[longest] + 1) % entries.shape[longest]] + spot[longest + 1:]
    return entries.at[tuple(spot)].set(low).at[tuple(neighbour)].set(largest)


def routed_block(key, own, number, rows, number_of, top, reach, skew):
    order = jax.random.permutation(key, number_of)
    crowded, usual = portions_of(number_of, rows * top, reach, skew, True), portions_of(number_of, rows * top, reach, skew, False)
    places = jnp.arange(number_of)

    def named(lengths, turn):
        used = int((lengths > 0).sum())
        fixed = max(1, used // 4)
        moved = fixed + (places - fixed + turn * (used - fixed)) % max(1, number_of - fixed)
        return jnp.zeros((number_of,), jnp.int32).at[order[jnp.where(places < fixed, places, moved)]].set(jnp.asarray(lengths, jnp.int32))

    lengths = jnp.where(number % 4 == 0, named(crowded, number // 4), named(usual, number - number // 4 - 1))
    mixed = jax.random.permutation(jax.random.fold_in(own, 3), number_of)
    source_of, receiver = mixed[0:number_of // 2 * 2:2], mixed[1:number_of // 2 * 2:2]
    margin = jnp.minimum(lengths[source_of] - 1, reach - lengths[receiver]) // 2
    margin = jnp.where((source_of == order[0]) | (receiver == order[0]) | (lengths[receiver] == 0), 0, jnp.maximum(margin, 0))
    moved = jax.random.randint(jax.random.fold_in(own, 4), (number_of // 2,), 0, 1 << 20) % (margin + 1)
    lengths = lengths.at[source_of].add(-moved).at[receiver].add(moved)
    members = jnp.searchsorted(jnp.cumsum(lengths), jnp.arange(rows * top), side="right").astype(jnp.int32)
    listing = members.reshape(top, rows).T
    listing = listing[jax.random.permutation(jax.random.fold_in(own, 1), rows)]
    turn = jax.random.randint(jax.random.fold_in(own, 2), (rows, 1), 0, top)
    return jnp.take_along_axis(listing, (jnp.arange(top)[None, :] + turn) % top, axis=1)


def portions_of(number_of, total, reach, lean, full):
    loads = [(1 << 20) // math.isqrt(rank ** lean) + 1 for rank in range(1, number_of + 1)]
    largest = reach if full else min(reach, max(-(-total // number_of), total * loads[0] // sum(loads)))
    least = 1 if total - largest >= number_of - 1 else 0
    holding, spare = [largest] + [least] * (number_of - 1), total - largest - least * (number_of - 1)
    while spare > 0:
        movable = [i for i in range(1, number_of) if holding[i] < largest] or [i for i in range(1, number_of) if holding[i] < reach]
        pool, budget = sum([loads[i] for i in movable]), spare
        for i in movable:
            addition = min(reach - holding[i], max(1, budget * loads[i] // pool), spare)
            holding[i] = holding[i] + addition
            spare = spare - addition
    return np.array(holding)


def setup_inputs(seed: int = 0) -> dict:
    key_list = jax.random.split(jax.random.key(seed), 6)
    spectra = draw_spectra(jax.random.fold_in(key_list[5], 71), 0)
    flags = place_ends((jax.random.randint(key_list[1], (STATIONS,), 0, 8) < 7).astype(jnp.int32), jax.random.fold_in(key_list[1], 1), 0, 1)
    pair_first = place_ends(jax.random.randint(key_list[2], (BLOCKS, BLOCKS, CAP), 0, ST_DEV), jax.random.fold_in(key_list[2], 1), 0, ST_DEV - 1).astype(jnp.int32)
    pair_second = place_ends(jax.random.randint(key_list[3], (BLOCKS, BLOCKS, CAP), 0, ST_DEV), jax.random.fold_in(key_list[3], 1), 0, ST_DEV - 1).astype(jnp.int32)
    owners_keys = jax.random.split(jax.random.fold_in(key_list[4], 1), BLOCKS * BLOCKS * CAP // (BLOCKS * CAP))
    owners_turns = jax.random.permutation(jax.random.fold_in(key_list[4], 3), BLOCKS * BLOCKS * CAP // (BLOCKS * CAP))
    owners = jax.vmap(lambda own, number: routed_block(jax.random.fold_in(key_list[4], 2), own, number, BLOCKS * CAP, BLOCKS, 1, CAPO, 2))(owners_keys, owners_turns).reshape((BLOCKS, BLOCKS, CAP, 1))
    return dict(spectra=spectra, flags=flags, pair_first=pair_first, pair_second=pair_second, owners=owners)


def whiten(raw, flags):
    values = raw.astype(jnp.float32)
    power = values[..., 0, :] ** 2 + values[..., 1, :] ** 2
    leading = power.shape[:-1]
    bands = lax.optimization_barrier(jnp.mean(power.reshape(leading + (F // BAND, BAND)), axis=-1))
    scales = jnp.repeat(lax.rsqrt(bands + 1e-06), BAND, axis=-1)
    alive = flags.astype(jnp.float32)
    return (values * scales[..., None, :] * alive[:, None, None]).astype(jnp.bfloat16)

def lag_table():
    freqs = jnp.arange(F, dtype=jnp.int32)
    shifts = jnp.arange(LAGS, dtype=jnp.int32) - LAGS // 2
    phase = freqs[:, None] * shifts[None, :] % (2 * F)
    theta = phase.astype(jnp.float32) * (math.pi / F)
    norm = 1.0 / math.sqrt(F)
    return (jnp.concatenate([jnp.cos(theta), -jnp.sin(theta)], axis=0) * norm).astype(jnp.bfloat16)

def cross(left, right):
    lvals = left.astype(jnp.float32)
    rvals = right.astype(jnp.float32)
    real = lvals[..., 0, :] * rvals[..., 0, :] + lvals[..., 1, :] * rvals[..., 1, :]
    imag = lvals[..., 1, :] * rvals[..., 0, :] - lvals[..., 0, :] * rvals[..., 1, :]
    return jnp.concatenate([real, imag], axis=-1).astype(jnp.bfloat16)

def reference(spectra, flags, pair_first, pair_second, owners):
    white = whiten(spectra, flags)
    table = lag_table().astype(jnp.float32)
    blocks = jnp.arange(BLOCKS, dtype=jnp.int32)

    def per_source(source):
        firsts = lax.dynamic_index_in_dim(pair_first, source, 0, keepdims=False)
        seconds = lax.dynamic_index_in_dim(pair_second, source, 0, keepdims=False)
        owner = lax.dynamic_index_in_dim(owners, source, 0, keepdims=False).reshape(-1)
        left_idx = (source * ST_DEV + firsts).reshape(-1).astype(jnp.int32)
        right_idx = (blocks[:, None] * ST_DEV + seconds).reshape(-1).astype(jnp.int32)
        spec_sum = lax.optimization_barrier(jnp.sum(cross(white[:, left_idx], white[:, right_idx]).astype(jnp.float32), axis=0))
        rows = jnp.dot(spec_sum, table, precision=lax.Precision.HIGHEST, preferred_element_type=jnp.float32)
        rows = rows * (1.0 / SEGS)
        chosen = (owner[:, None] == blocks[None, :]).astype(jnp.int32)
        before = jnp.cumsum(chosen, axis=0) - chosen
        rank = lax.optimization_barrier(jnp.sum(before * chosen, axis=1)).astype(jnp.int32)
        return jnp.zeros((BLOCKS, CAPO, LAGS), jnp.float32).at[owner, rank].set(rows)
    stacked = lax.map(per_source, blocks)
    return jnp.transpose(stacked, (1, 0, 2, 3))
```

```python
import functools
import math

import jax
import jax.numpy as jnp
import numpy as np
from jax import lax
from jax.experimental import pallas as pl
from jax.experimental.pallas import tpu as pltpu
from jax.sharding import PartitionSpec as P

F = 4096
LAGS = 1024
BAND = 64
CAPO = 8
COLS = 1024
PARTS = F // COLS
ROWS = 4 * PARTS
LO = 2
CORES = 2


def lag_table(segs):
    freqs = np.arange(F, dtype=np.int64)
    shifts = np.arange(LAGS, dtype=np.int64) - LAGS // 2
    phase = freqs[:, None] * shifts[None, :] % (2 * F)
    angles = np.arange(2 * F) * (math.pi / F)
    norm = 1.0 / math.sqrt(F)
    cosines = (np.cos(angles) * norm).astype(np.float32).astype(jnp.bfloat16)
    sines = (-np.sin(angles) * norm).astype(np.float32).astype(jnp.bfloat16)
    whole = np.concatenate([cosines[phase], sines[phase]], axis=0)
    return np.ascontiguousarray(whole.reshape(2 * F, segs, LAGS // segs).transpose(1, 0, 2))


def position(core, lo, hi, his):
    return (core * LO + lo) * his + hi


def kernel(
    blocks, segs, cap,
    spectra_ref, flags_ref, meta_ref, table_ref, out_ref,
    buf, mbuf, tbl, sel, re_ref, im_ref,
    ssem, rsem, msend, mrecv, tsem,
):
    his = blocks // (LO * CORES)
    rank_out = blocks * CAPO
    depth = blocks * ROWS
    width = mbuf.shape[-1]
    stn = lax.axis_index("stn")
    seg = lax.axis_index("seg")
    core = lax.rem(stn, CORES)
    lo = lax.rem(stn // CORES, LO)
    hi = stn // (CORES * LO)
    mypos = position(core, lo, hi, his)

    def device(core, lo, hi, seg):
        return ((hi * LO + lo) * CORES + core, seg)

    z_peers = [lax.rem(hi + d, his) for d in range(1, his)]
    x_peers = [lax.rem(seg + d, segs) for d in range(1, segs)]
    z_ids = [device(core, lo, h, seg) for h in z_peers]
    x_ids = [device(core, lo, hi, s) for s in x_peers]
    y_id = device(core, 1 - lo, hi, seg)
    c_id = device(1 - core, lo, hi, seg)
    mesh_id = pl.DeviceIdType.MESH

    barrier = pltpu.get_barrier_semaphore()
    partners = z_ids + x_ids + [y_id, c_id]
    for partner in partners:
        pl.semaphore_signal(barrier, inc=1, device_id=partner, device_id_type=mesh_id)
    table_copy = pltpu.make_async_copy(table_ref.at[seg], tbl, tsem)
    table_copy.start()

    for st in range(2):
        for p in range(PARTS):
            span = pl.ds(p * COLS, COLS)
            row = pl.ds(st * PARTS + p, 1)
            re_ref[row, :] = spectra_ref[0, st, 0:1, span].astype(jnp.float32)
            im_ref[row, :] = spectra_ref[0, st, 1:2, span].astype(jnp.float32)
    re = re_ref[...]
    im = im_ref[...]
    power = re * re + im * im
    lanes = 128
    stacked = jnp.concatenate(
        [power[:, k * lanes:(k + 1) * lanes] for k in range(COLS // lanes)], axis=0
    )
    left = lax.broadcasted_iota(jnp.int32, (lanes, lanes), 0) // BAND
    right = lax.broadcasted_iota(jnp.int32, (lanes, lanes), 1) // BAND
    ones = (left == right).astype(jnp.float32)
    sums = jnp.dot(
        stacked, ones, precision=lax.Precision.HIGHEST, preferred_element_type=jnp.float32
    )
    scales = lax.rsqrt(sums * (1.0 / BAND) + 1e-06)
    per = 2 * PARTS
    scales = jnp.concatenate(
        [scales[k * per:(k + 1) * per] for k in range(COLS // lanes)], axis=1
    )
    station = lax.broadcasted_iota(jnp.int32, (per, COLS), 0) // PARTS
    alive = jnp.where(station == 0, flags_ref[0], flags_ref[1]).astype(jnp.float32)
    white = jnp.concatenate([re * scales * alive, im * scales * alive], axis=0)
    buf[seg, mypos] = white.astype(jnp.bfloat16)
    mbuf[mypos] = meta_ref[...]

    pl.semaphore_wait(barrier, len(partners))

    def data(g, pos, k, target):
        return pltpu.make_async_remote_copy(
            src_ref=buf.at[g, pos], dst_ref=buf.at[g, pos],
            send_sem=ssem.at[k], recv_sem=rsem.at[g, pos],
            device_id=target, device_id_type=mesh_id,
        )

    def forward(g, pos, k, targets):
        for target in targets:
            data(g, pos, k, target).start()
            k += 1
        return k

    def arrived(g, pos):
        data(g, pos, 0, c_id).wait_recv()

    def meta(start, count, k, recv, target):
        part = mbuf.at[pl.ds(start, count)]
        return pltpu.make_async_remote_copy(
            src_ref=part, dst_ref=part, send_sem=msend.at[k], recv_sem=mrecv.at[recv],
            device_id=target, device_id_type=mesh_id,
        )

    for d, target in enumerate(z_ids):
        meta(mypos, 1, d, d, target).start()
    k = forward(seg, mypos, 0, z_ids + x_ids + [y_id, c_id])
    froms = [lax.rem(hi + his - d, his) for d in range(1, his)]
    for d, h in enumerate(froms):
        meta(position(core, lo, h, his), 1, d, d, c_id).wait_recv()
    first = position(core, lo, 0, his)
    meta(first, his, his - 1, his - 1, y_id).start()
    for h in froms:
        pos = position(core, lo, h, his)
        arrived(seg, pos)
        k = forward(seg, pos, k, x_ids + [y_id, c_id])
    base = k
    meta(position(core, 1 - lo, 0, his), his, 0, his - 1, c_id).wait_recv()
    half = position(core, 0, 0, his)
    meta(half, LO * his, his, his, c_id).start()

    second_count = {0: 2 * his * (segs - 1), 1: his * segs}

    @pl.when(core == 0)
    def _():
        k = base
        for s in x_peers:
            for h in range(his):
                pos = position(0, lo, h, his)
                arrived(s, pos)
                k = forward(s, pos, k, [y_id, c_id])
        assert k - base == second_count[0]

    @pl.when(core == 1)
    def _():
        k = base
        for h in range(his):
            pos = position(1, 1 - lo, h, his)
            arrived(seg, pos)
            k = forward(seg, pos, k, x_ids + [c_id])
        assert k - base == second_count[1]

    meta(position(1 - core, 0, 0, his), LO * his, 0, his, c_id).wait_recv()
    firsts = mbuf[:, 0, :]
    seconds = mbuf[:, 1, :]
    owner = mbuf[:, 2, :]
    pair = lax.broadcasted_iota(jnp.int32, (blocks, width), 1)
    block = pair // cap
    block_pos = position(
        block % CORES, (block // CORES) % LO, block // (CORES * LO), his
    )
    source_pos = lax.broadcasted_iota(jnp.int32, (blocks, width), 0)
    offset = 4096
    left_row = (source_pos * ROWS + firsts * PARTS + offset).astype(jnp.float32)
    right_row = (block_pos * ROWS + seconds * PARTS + offset).astype(jnp.float32)
    mine = (owner == stn).astype(jnp.float32)
    before = (
        lax.broadcasted_iota(jnp.int32, (width, width), 0)
        < lax.broadcasted_iota(jnp.int32, (width, width), 1)
    ).astype(jnp.float32)
    rank = jnp.dot(mine, before, preferred_element_type=jnp.float32)
    slot = lax.broadcasted_iota(jnp.int32, (blocks, CAPO, width), 1).astype(jnp.float32)
    taken = jnp.where(rank[:, None, :] == slot, mine[:, None, :], 0.0)
    left_at = jnp.sum(taken * left_row[:, None, :], axis=2, keepdims=True)
    right_at = jnp.sum(taken * right_row[:, None, :], axis=2, keepdims=True)
    picks = jnp.concatenate(
        [left_at.reshape(rank_out, 1), right_at.reshape(rank_out, 1)], axis=0
    ).astype(jnp.int32) - offset
    column = lax.broadcasted_iota(jnp.int32, (2 * rank_out, depth), 1)
    gap = column - picks
    for c in range(2):
        for p in range(PARTS):
            hit = gap == c * 2 * PARTS + p
            sel[c * PARTS + p] = jnp.where(hit, 1.0, 0.0).astype(jnp.bfloat16)

    third_base = base + max(second_count.values())

    @pl.when(core == 0)
    def _():
        k = third_base
        for s in [seg] + x_peers:
            for h in range(his):
                pos = position(0, 1 - lo, h, his)
                arrived(s, pos)
                k = forward(s, pos, k, [c_id])

    @pl.when(core == 1)
    def _():
        k = third_base
        for s in x_peers:
            for l in (lo, 1 - lo):
                for h in range(his):
                    pos = position(1, l, h, his)
                    arrived(s, pos)
                    k = forward(s, pos, k, [c_id])

    for s in [seg] + x_peers:
        for l in range(LO):
            for h in range(his):
                arrived(s, position(1 - core, l, h, his))

    table_copy.wait()
    total = jnp.zeros((rank_out, out_ref.shape[-1]), jnp.float32)
    for p in range(PARTS):
        real = imag = None
        for g in range(segs):
            white = buf[g].reshape(depth, COLS)
            a = jnp.dot(sel[p], white, preferred_element_type=jnp.float32)
            b = jnp.dot(sel[PARTS + p], white, preferred_element_type=jnp.float32)
            ar, br = a[:rank_out], a[rank_out:]
            ai, bi = b[:rank_out], b[rank_out:]
            r = ar * br + ai * bi
            i = ai * br - ar * bi
            real = r if g == 0 else real + r
            imag = i if g == 0 else imag + i
        total += jnp.dot(
            real.astype(jnp.bfloat16), tbl[pl.ds(p * COLS, COLS)],
            preferred_element_type=jnp.float32,
        )
        total += jnp.dot(
            imag.astype(jnp.bfloat16), tbl[pl.ds(F + p * COLS, COLS)],
            preferred_element_type=jnp.float32,
        )
    total = total * (1.0 / segs)
    for b in range(blocks):
        pos = position(b % CORES, (b // CORES) % LO, b // (CORES * LO), his)
        out_ref[0, b] = total[pos * CAPO:(pos + 1) * CAPO]

    for d in range(his - 1):
        meta(0, 1, d, d, c_id).wait_send()
    meta(0, his, his - 1, 0, c_id).wait_send()
    meta(0, LO * his, his, 0, c_id).wait_send()

    def sent(start, count):
        for k in range(start, start + count):
            data(0, 0, k, c_id).wait_send()

    sent(0, base)

    @pl.when(core == 0)
    def _():
        sent(base, second_count[0])
        sent(third_base, his * segs)

    @pl.when(core == 1)
    def _():
        sent(base, second_count[1])
        sent(third_base, LO * his * (segs - 1))


def shards(blocks, segs, table, spectra, flags, pair_first, pair_second, owners):
    his = blocks // (LO * CORES)
    cap = pair_first.shape[-1]
    pairs = blocks * cap
    width = -(-pairs // 128) * 128
    lists = jnp.stack(
        [pair_first.reshape(pairs), pair_second.reshape(pairs), owners.reshape(pairs)]
    )
    lists = jnp.pad(lists, ((0, 5), (0, width - pairs)), constant_values=-1)
    lags = LAGS // segs
    slots = blocks * CAPO
    copies = (his - 1) + segs + 1 + (his - 1) * (segs + 1)
    copies += max(2 * his * (segs - 1), his * segs)
    copies += max(his * segs, LO * his * (segs - 1))
    vmem = pl.BlockSpec(memory_space=pltpu.VMEM)
    return pl.pallas_call(
        functools.partial(kernel, blocks, segs, cap),
        out_shape=jax.ShapeDtypeStruct((1, blocks, CAPO, lags), jnp.float32),
        in_specs=[
            vmem,
            pl.BlockSpec(memory_space=pltpu.SMEM),
            vmem,
            pl.BlockSpec(memory_space=pl.ANY),
        ],
        out_specs=vmem,
        scratch_shapes=[
            pltpu.VMEM((segs, blocks, ROWS, COLS), jnp.bfloat16),
            pltpu.VMEM((blocks, 8, width), jnp.int32),
            pltpu.VMEM((2 * F, lags), jnp.bfloat16),
            pltpu.VMEM((2 * PARTS, 2 * slots, blocks * ROWS), jnp.bfloat16),
            pltpu.VMEM((2 * PARTS, COLS), jnp.float32),
            pltpu.VMEM((2 * PARTS, COLS), jnp.float32),
            pltpu.SemaphoreType.DMA((copies,)),
            pltpu.SemaphoreType.DMA((segs, blocks)),
            pltpu.SemaphoreType.DMA((his + 1,)),
            pltpu.SemaphoreType.DMA((his + 1,)),
            pltpu.SemaphoreType.DMA,
        ],
        compiler_params=pltpu.CompilerParams(
            collective_id=0, has_side_effects=True, vmem_limit_bytes=48 * 1024 * 1024
        ),
        cost_estimate=pl.CostEstimate(
            flops=4 * slots * F * lags, bytes_accessed=4 * F * lags, transcendentals=0
        ),
    )(spectra, flags, lists, table)


def solution(mesh):
    blocks = mesh.shape["stn"]
    segs = mesh.shape["seg"]
    table = lag_table(segs)

    def program(spectra, flags, pair_first, pair_second, owners):
        return jax.shard_map(
            functools.partial(shards, blocks, segs, table),
            mesh=mesh,
            in_specs=(
                P("seg", "stn", None, None),
                P("stn"),
                P("stn", None, None),
                P("stn", None, None),
                P("stn", None, None, None),
            ),
            out_specs=P("stn", None, None, "seg"),
            check_vma=False,
        )(spectra, flags, pair_first, pair_second, owners)

    return program
```

```python
import functools
import math

import jax
import jax.numpy as jnp
import numpy as np
from jax import lax
from jax.experimental import pallas as pl
from jax.experimental.pallas import tpu as pltpu
from jax.sharding import PartitionSpec as P

F = 4096
LAGS = 1024
BAND = 64
CAPO = 8
COLS = 1024
PARTS = F // COLS
ROWS = 4 * PARTS
LO = 2
CORES = 2


def lag_table(segs):
    freqs = np.arange(F, dtype=np.int64)
    shifts = np.arange(LAGS, dtype=np.int64) - LAGS // 2
    phase = freqs[:, None] * shifts[None, :] % (2 * F)
    angles = np.arange(2 * F) * (math.pi / F)
    norm = 1.0 / math.sqrt(F)
    cosines = (np.cos(angles) * norm).astype(np.float32).astype(jnp.bfloat16)
    sines = (-np.sin(angles) * norm).astype(np.float32).astype(jnp.bfloat16)
    whole = np.concatenate([cosines[phase], sines[phase]], axis=0)
    return np.ascontiguousarray(whole.reshape(2 * F, segs, LAGS // segs).transpose(1, 0, 2))


def position(core, lo, hi, his):
    return (core * LO + lo) * his + hi


def kernel(
    blocks, segs, cap,
    spectra_hbm, flags_hbm, firsts_hbm, seconds_hbm, owners_hbm, table_ref, out_ref,
    spectra_ref, flags_ref, firsts_ref, seconds_ref, owners_ref,
    buf, mbuf, tbl, sel, re_ref, im_ref,
    ssem, rsem, msend, mrecv, tsem, isem,
):
    his = blocks // (LO * CORES)
    rank_out = blocks * CAPO
    depth = blocks * ROWS
    width = mbuf.shape[-1]
    stn = lax.axis_index("stn")
    seg = lax.axis_index("seg")
    core = lax.rem(stn, CORES)
    lo = lax.rem(stn // CORES, LO)
    hi = stn // (CORES * LO)
    mypos = position(core, lo, hi, his)

    def device(core, lo, hi, seg):
        return ((hi * LO + lo) * CORES + core, seg)

    z_peers = [lax.rem(hi + d, his) for d in range(1, his)]
    x_peers = [lax.rem(seg + d, segs) for d in range(1, segs)]
    z_ids = [device(core, lo, h, seg) for h in z_peers]
    x_ids = [device(core, lo, hi, s) for s in x_peers]
    y_id = device(core, 1 - lo, hi, seg)
    c_id = device(1 - core, lo, hi, seg)
    mesh_id = pl.DeviceIdType.MESH

    inputs = [
        pltpu.make_async_copy(source, target, isem.at[n])
        for n, (source, target) in enumerate((
            (spectra_hbm, spectra_ref), (flags_hbm, flags_ref), (firsts_hbm, firsts_ref),
            (seconds_hbm, seconds_ref), (owners_hbm, owners_ref),
        ))
    ]
    for copy in inputs:
        copy.start()
    barrier = pltpu.get_barrier_semaphore()
    partners = z_ids + x_ids + [y_id, c_id]
    for partner in partners:
        pl.semaphore_signal(barrier, inc=1, device_id=partner, device_id_type=mesh_id)
    table_copy = pltpu.make_async_copy(table_ref.at[seg], tbl, tsem)
    table_copy.start()

    for copy in inputs:
        copy.wait()

    for st in range(2):
        for p in range(PARTS):
            span = pl.ds(p * COLS, COLS)
            row = pl.ds(st * PARTS + p, 1)
            re_ref[row, :] = spectra_ref[0, st, 0:1, span].astype(jnp.float32)
            im_ref[row, :] = spectra_ref[0, st, 1:2, span].astype(jnp.float32)
    re = re_ref[...]
    im = im_ref[...]
    power = re * re + im * im
    lanes = 128
    stacked = jnp.concatenate(
        [power[:, k * lanes:(k + 1) * lanes] for k in range(COLS // lanes)], axis=0
    )
    left = lax.broadcasted_iota(jnp.int32, (lanes, lanes), 0) // BAND
    right = lax.broadcasted_iota(jnp.int32, (lanes, lanes), 1) // BAND
    ones = (left == right).astype(jnp.float32)
    sums = jnp.dot(
        stacked, ones, precision=lax.Precision.HIGHEST, preferred_element_type=jnp.float32
    )
    scales = lax.rsqrt(sums * (1.0 / BAND) + 1e-06)
    per = 2 * PARTS
    scales = jnp.concatenate(
        [scales[k * per:(k + 1) * per] for k in range(COLS // lanes)], axis=1
    )
    station = lax.broadcasted_iota(jnp.int32, (per, COLS), 0) // PARTS
    alive = jnp.where(station == 0, flags_ref[0], flags_ref[1]).astype(jnp.float32)
    white = jnp.concatenate([re * scales * alive, im * scales * alive], axis=0)
    buf[seg, mypos] = white.astype(jnp.bfloat16)

    spread = (
        lax.broadcasted_iota(jnp.int32, (blocks, width), 1) % blocks
        == lax.broadcasted_iota(jnp.int32, (blocks, width), 0)
    ).astype(jnp.float32)
    lane = lax.broadcasted_iota(jnp.int32, (cap, width), 1)
    keep = lane // blocks == lax.broadcasted_iota(jnp.int32, (cap, width), 0)

    def flat(listed):
        tiled = jnp.dot(
            listed.astype(jnp.float32), spread, preferred_element_type=jnp.float32
        )
        return jnp.sum(jnp.where(keep, tiled, 0.0), axis=0, keepdims=True).astype(jnp.int32)

    inside = lax.broadcasted_iota(jnp.int32, (1, width), 1) < blocks * cap
    mbuf[mypos, 0:1] = flat(firsts_ref[0])
    mbuf[mypos, 1:2] = flat(seconds_ref[0])
    mbuf[mypos, 2:3] = jnp.where(inside, flat(owners_ref[0, :, 0]), -1)

    pl.semaphore_wait(barrier, len(partners))

    def data(g, pos, k, target):
        return pltpu.make_async_remote_copy(
            src_ref=buf.at[g, pos], dst_ref=buf.at[g, pos],
            send_sem=ssem.at[k], recv_sem=rsem.at[g, pos],
            device_id=target, device_id_type=mesh_id,
        )

    def forward(g, pos, k, targets):
        for target in targets:
            data(g, pos, k, target).start()
            k += 1
        return k

    def arrived(g, pos):
        data(g, pos, 0, c_id).wait_recv()

    def meta(start, count, k, recv, target):
        part = mbuf.at[pl.ds(start, count)]
        return pltpu.make_async_remote_copy(
            src_ref=part, dst_ref=part, send_sem=msend.at[k], recv_sem=mrecv.at[recv],
            device_id=target, device_id_type=mesh_id,
        )

    for d, target in enumerate(z_ids):
        meta(mypos, 1, d, d, target).start()
    k = forward(seg, mypos, 0, z_ids + x_ids + [y_id, c_id])
    froms = [lax.rem(hi + his - d, his) for d in range(1, his)]
    for d, h in enumerate(froms):
        meta(position(core, lo, h, his), 1, d, d, c_id).wait_recv()
    first = position(core, lo, 0, his)
    meta(first, his, his - 1, his - 1, y_id).start()
    for h in froms:
        pos = position(core, lo, h, his)
        arrived(seg, pos)
        k = forward(seg, pos, k, x_ids + [y_id, c_id])
    base = k
    meta(position(core, 1 - lo, 0, his), his, 0, his - 1, c_id).wait_recv()
    half = position(core, 0, 0, his)
    meta(half, LO * his, his, his, c_id).start()

    second_count = {0: 2 * his * (segs - 1), 1: his * segs}

    @pl.when(core == 0)
    def _():
        k = base
        for s in x_peers:
            for h in range(his):
                pos = position(0, lo, h, his)
                arrived(s, pos)
                k = forward(s, pos, k, [y_id, c_id])
        assert k - base == second_count[0]

    @pl.when(core == 1)
    def _():
        k = base
        for h in range(his):
            pos = position(1, 1 - lo, h, his)
            arrived(seg, pos)
            k = forward(seg, pos, k, x_ids + [c_id])
        assert k - base == second_count[1]

    meta(position(1 - core, 0, 0, his), LO * his, 0, his, c_id).wait_recv()
    firsts = mbuf[:, 0, :]
    seconds = mbuf[:, 1, :]
    owner = mbuf[:, 2, :]
    pair = lax.broadcasted_iota(jnp.int32, (blocks, width), 1)
    block = pair % blocks
    block_pos = position(
        block % CORES, (block // CORES) % LO, block // (CORES * LO), his
    )
    source_pos = lax.broadcasted_iota(jnp.int32, (blocks, width), 0)
    offset = 4096
    left_row = (source_pos * ROWS + firsts * PARTS + offset).astype(jnp.float32)
    right_row = (block_pos * ROWS + seconds * PARTS + offset).astype(jnp.float32)
    mine = (owner == stn).astype(jnp.float32)
    one = lax.broadcasted_iota(jnp.int32, (width, width), 0)
    two = lax.broadcasted_iota(jnp.int32, (width, width), 1)
    before = (
        one % blocks * cap + one // blocks < two % blocks * cap + two // blocks
    ).astype(jnp.float32)
    rank = jnp.dot(mine, before, preferred_element_type=jnp.float32)
    slot = lax.broadcasted_iota(jnp.int32, (blocks, CAPO, width), 1).astype(jnp.float32)
    taken = jnp.where(rank[:, None, :] == slot, mine[:, None, :], 0.0)
    left_at = jnp.sum(taken * left_row[:, None, :], axis=2, keepdims=True)
    right_at = jnp.sum(taken * right_row[:, None, :], axis=2, keepdims=True)
    picks = jnp.concatenate(
        [left_at.reshape(rank_out, 1), right_at.reshape(rank_out, 1)], axis=0
    ).astype(jnp.int32) - offset
    column = lax.broadcasted_iota(jnp.int32, (2 * rank_out, depth), 1)
    gap = column - picks
    for c in range(2):
        for p in range(PARTS):
            hit = gap == c * 2 * PARTS + p
            sel[c * PARTS + p] = jnp.where(hit, 1.0, 0.0).astype(jnp.bfloat16)

    third_base = base + max(second_count.values())

    @pl.when(core == 0)
    def _():
        k = third_base
        for s in [seg] + x_peers:
            for h in range(his):
                pos = position(0, 1 - lo, h, his)
                arrived(s, pos)
                k = forward(s, pos, k, [c_id])

    @pl.when(core == 1)
    def _():
        k = third_base
        for s in x_peers:
            for l in (lo, 1 - lo):
                for h in range(his):
                    pos = position(1, l, h, his)
                    arrived(s, pos)
                    k = forward(s, pos, k, [c_id])

    for s in [seg] + x_peers:
        for l in range(LO):
            for h in range(his):
                arrived(s, position(1 - core, l, h, his))

    table_copy.wait()
    total = jnp.zeros((rank_out, out_ref.shape[-1]), jnp.float32)
    for p in range(PARTS):
        real = imag = None
        for g in range(segs):
            white = buf[g].reshape(depth, COLS)
            a = jnp.dot(sel[p], white, preferred_element_type=jnp.float32)
            b = jnp.dot(sel[PARTS + p], white, preferred_element_type=jnp.float32)
            ar, br = a[:rank_out], a[rank_out:]
            ai, bi = b[:rank_out], b[rank_out:]
            r = ar * br + ai * bi
            i = ai * br - ar * bi
            real = r if g == 0 else real + r
            imag = i if g == 0 else imag + i
        total += jnp.dot(
            real.astype(jnp.bfloat16), tbl[pl.ds(p * COLS, COLS)],
            preferred_element_type=jnp.float32,
        )
        total += jnp.dot(
            imag.astype(jnp.bfloat16), tbl[pl.ds(F + p * COLS, COLS)],
            preferred_element_type=jnp.float32,
        )
    total = total * (1.0 / segs)
    for b in range(blocks):
        pos = position(b % CORES, (b // CORES) % LO, b // (CORES * LO), his)
        out_ref[0, b] = total[pos * CAPO:(pos + 1) * CAPO]

    for d in range(his - 1):
        meta(0, 1, d, d, c_id).wait_send()
    meta(0, his, his - 1, 0, c_id).wait_send()
    meta(0, LO * his, his, 0, c_id).wait_send()

    def sent(start, count):
        for k in range(start, start + count):
            data(0, 0, k, c_id).wait_send()

    sent(0, base)

    @pl.when(core == 0)
    def _():
        sent(base, second_count[0])
        sent(third_base, his * segs)

    @pl.when(core == 1)
    def _():
        sent(base, second_count[1])
        sent(third_base, LO * his * (segs - 1))


def shards(blocks, segs, table, spectra, flags, pair_first, pair_second, owners):
    his = blocks // (LO * CORES)
    cap = pair_first.shape[-1]
    pairs = blocks * cap
    width = -(-pairs // 128) * 128
    lags = LAGS // segs
    slots = blocks * CAPO
    copies = (his - 1) + segs + 1 + (his - 1) * (segs + 1)
    copies += max(2 * his * (segs - 1), his * segs)
    copies += max(his * segs, LO * his * (segs - 1))
    vmem = pl.BlockSpec(memory_space=pltpu.VMEM)
    return pl.pallas_call(
        functools.partial(kernel, blocks, segs, cap),
        out_shape=jax.ShapeDtypeStruct((1, blocks, CAPO, lags), jnp.float32),
        in_specs=[pl.BlockSpec(memory_space=pltpu.HBM)] * 6,
        out_specs=vmem,
        scratch_shapes=[
            pltpu.VMEM(spectra.shape, jnp.bfloat16),
            pltpu.SMEM(flags.shape, jnp.int32),
            pltpu.VMEM((1, cap, blocks), jnp.int32),
            pltpu.VMEM((1, cap, blocks), jnp.int32),
            pltpu.VMEM((1, cap, 1, blocks), jnp.int32),
            pltpu.VMEM((segs, blocks, ROWS, COLS), jnp.bfloat16),
            pltpu.VMEM((blocks, 8, width), jnp.int32),
            pltpu.VMEM((2 * F, lags), jnp.bfloat16),
            pltpu.VMEM((2 * PARTS, 2 * slots, blocks * ROWS), jnp.bfloat16),
            pltpu.VMEM((2 * PARTS, COLS), jnp.float32),
            pltpu.VMEM((2 * PARTS, COLS), jnp.float32),
            pltpu.SemaphoreType.DMA((copies,)),
            pltpu.SemaphoreType.DMA((segs, blocks)),
            pltpu.SemaphoreType.DMA((his + 1,)),
            pltpu.SemaphoreType.DMA((his + 1,)),
            pltpu.SemaphoreType.DMA,
            pltpu.SemaphoreType.DMA((5,)),
        ],
        compiler_params=pltpu.CompilerParams(
            collective_id=0, has_side_effects=True, vmem_limit_bytes=48 * 1024 * 1024
        ),
        cost_estimate=pl.CostEstimate(
            flops=4 * slots * F * lags, bytes_accessed=4 * F * lags, transcendentals=0
        ),
    )(
        spectra, flags, pair_first.transpose(0, 2, 1), pair_second.transpose(0, 2, 1),
        owners.transpose(0, 2, 3, 1), table,
    )


def solution(mesh):
    blocks = mesh.shape["stn"]
    segs = mesh.shape["seg"]
    table = lag_table(segs)

    def program(spectra, flags, pair_first, pair_second, owners):
        return jax.shard_map(
            functools.partial(shards, blocks, segs, table),
            mesh=mesh,
            in_specs=(
                P("seg", "stn", None, None),
                P("stn"),
                P("stn", None, None),
                P("stn", None, None),
                P("stn", None, None, None),
            ),
            out_specs=P("stn", None, None, "seg"),
            check_vma=False,
        )(spectra, flags, pair_first, pair_second, owners)

    return program
```
